32 devices in a mesh: dom: 32 (over z, y, x, core).
Axes of the slice: x: 2, y: 2, z: 4, core: 2. Of those that a mesh axis runs over, the one named last changes fastest.
Arguments:
- features: bfloat16 [32768, 768], P('dom'), may hold values from -6 to 6
- w_self: bfloat16 [768, 1024], replicated, may hold values from -0.21875 to 0.21875
- w_neigh: bfloat16 [768, 1024], replicated, may hold values from -0.875 to 0.875
- cotangent: bfloat16 [32768, 1024], P('dom'), may hold values from -6 to 6
- tiles: bfloat16 [256, 8, 128, 128], P('dom'), may hold values from 0 to 1, as said below
- tile_src: int32 [256, 8], P('dom'), may hold values from 0 to 12, as said below
- tile_count: int32 [256], P('dom'), may hold values from 1 to 8
- send_rows: int32 [32, 32, 16], P('dom'), may hold values from 0 to 1023
- send_count: int32 [32, 32], P('dom'), may hold values from 0 to 16, as said below
- hub_rows: int32 [32, 4], P('dom'), may hold values from 0 to 1023
Outputs:
- layer_out: bfloat16 [32768, 1024], P('dom')
- grad_features: float32 [32768, 768], P('dom')
- grad_w_self: float32 [768, 1024], P('dom')
- grad_w_neigh: float32 [768, 1024], P('dom')
The draws below stay inside these ranges and needn't reach their ends.
Inputs may be any that keep to these rules, and one draw needn't show every extreme that they name: `tile_src`: slot 0 of each block names the block itself (block t mod 1024/128 of the own rows); other slots name any block of the source table. `send_count`: A partition sends nothing to itself. `tiles`: Nonnegative; slot 0 of every block has a positive diagonal.
All inputs are finite; a program needn't handle non-finite values.
Results may differ from the reference program's by a relative error of at most 0.0052.
Values may be sent and summed in bfloat16 or wider, within the bound.
No kernel may reach another device: no remote copies, remote signals or barrier semaphores. Data moves between devices by JAX's collectives and lax.ppermute only.
A program may use at most 128 MiB of HBM per device.

```python
import jax
import jax.numpy as jnp
from jax import lax

F = 768
H = 1024
TILE = 128
TMAX = 8
ROWS_DEV = 1024
BND_DEV = 512
HUB = 128
CAP = 16
HUB_DEV = 4
NODES = 32768
BLOCKS = 256
N_DOM = 32


def draw_tile_src(key, part):
    key = jax.random.fold_in(key, 11)
    blocks_own = ROWS_DEV // TILE
    sources = (ROWS_DEV + BND_DEV + HUB) // TILE
    picks = jax.random.randint(key, (BLOCKS, TMAX), 0, sources, dtype=jnp.int32)
    block_ids = jnp.arange(BLOCKS, dtype=jnp.int32) % blocks_own
    picks = picks.at[:, 0].set(block_ids)
    first = block_ids == 0
    picks = picks.at[:, 1].set(jnp.where(first, sources - 1, picks[:, 1]))
    return picks


def draw_tile_count(key, part):
    key = jax.random.fold_in(key, 12)
    key_base, key_heavy = jax.random.split(key)
    blocks_own = ROWS_DEV // TILE
    base = jax.random.randint(key_base, (BLOCKS,), 1, TMAX + 1, dtype=jnp.int32)
    heavy = jax.random.randint(key_heavy, (N_DOM,), 0, 4, dtype=jnp.int32) == 0
    heavy = heavy.at[0].set(True)
    heavy_rows = jnp.repeat(heavy, blocks_own)
    return jnp.where(heavy_rows, TMAX, base).astype(jnp.int32)


def draw_send_count(key, part):
    key = jax.random.fold_in(key, 13)
    counts = jax.random.randint(key, (N_DOM, N_DOM), 0, CAP + 1, dtype=jnp.int32)
    owners = jnp.arange(N_DOM, dtype=jnp.int32)
    counts = jnp.where(owners[:, None] == owners[None, :], 0, counts)
    counts = counts.at[owners, (owners + 1) % N_DOM].set(CAP)
    return counts.astype(jnp.int32)


def draw_tiles(key, part):
    key = jax.random.fold_in(key, 14)
    key_mask, key_vals, key_diag = jax.random.split(key, 3)
    shape = (BLOCKS, TMAX, TILE, TILE)
    present = jax.random.bernoulli(key_mask, 0.125, shape).astype(jnp.float32)
    values = jnp.exp(jax.random.uniform(key_vals, shape, jnp.float32, jnp.log(0.05), 0.0))
    diag_vals = jnp.exp(jax.random.uniform(key_diag, (BLOCKS, TILE), jnp.float32, jnp.log(0.05), 0.0))
    eye = jnp.eye(TILE, dtype=jnp.float32)
    slot_zero = (jnp.arange(TMAX) == 0).astype(jnp.float32)
    diagonal = eye[None, None] * diag_vals[:, None, :, None] * slot_zero[None, :, None, None]
    return jnp.minimum(present * values + diagonal, 1.0).astype(jnp.bfloat16)


def with_ends(entries, rng, low, largest):
    shape = entries.shape
    place = [jax.random.randint(jax.random.fold_in(rng, axis), (), 0, shape[axis]) for axis in range(len(shape))]
    entries = entries.at[tuple(place)].set(low)
    longest = shape.index(max(shape))
    place[longest] = (place[longest] + 1) % shape[longest]
    return entries.at[tuple(place)].set(largest)


def raised(array, key, source, target, shards_of, factor):
    owner, partner = [(jnp.arange(array.shape[axis_at]) // (array.shape[axis_at] // shards_of)).reshape([-1 if axis == axis_at else 1 for axis in range(array.ndim)]) for axis_at in (source, target)]
    chosen = jax.random.permutation(key, shards_of)[partner]
    strong = (owner == chosen) | (owner == (partner + shards_of // 2) % shards_of)
    return jnp.where(strong, factor * array, array)


def level_of(stream_key, dims, cuts, smallest, largest):
    def one(dim, parts):
        heights = jax.random.uniform(jax.random.fold_in(jax.random.fold_in(stream_key, 6), dim), (parts,), jnp.float32, smallest / len(cuts), largest / len(cuts))
        return jnp.repeat(jnp.exp(heights), dims[dim] // parts).reshape((-1,) + (1,) * (len(dims) - dim - 1))

    level = one(*cuts[0])
    for cut in cuts[1:]:
        level = level * one(*cut)
    return level


def centred(stream_key, extent, spread, bound, shards=(), kind=jnp.bfloat16):
    drawn = spread * jax.random.normal(stream_key, extent, jnp.float32)
    if shards:
        drawn = drawn * level_of(stream_key, extent, shards, -0.22, 0.18)
    return jnp.clip(drawn, -bound, bound).astype(kind)


def heavy_noise(key, dims, spread, bound, shards, heavy, kind=jnp.bfloat16):
    entries = spread * jax.random.normal(key, dims, jnp.float32)
    if shards:
        entries = entries * level_of(key, dims, shards, -0.22, 0.18)
    return jnp.clip(raised(entries, jax.random.fold_in(key, 3), *heavy), -bound, bound).astype(kind)


def setup_inputs(seed: int = 0) -> dict:
    key_of = jax.random.split(jax.random.key(seed), 11)
    return {
        "features": heavy_noise(key_of[0], (NODES, F), 1.0, 6.0, ((0, 32),), (0, 1, 32, 2.75)),
        "w_self": centred(key_of[1], (F, H), F ** -0.5, 0.21875),
        "w_neigh": centred(key_of[2], (F, H), (F // 16) ** -0.5, 0.875),
        "cotangent": centred(key_of[3], (NODES, H), 1.0, 6.0, ((0, 32),)),
        "tiles": draw_tiles(jax.random.fold_in(key_of[10], 71), 0),
        "tile_src": draw_tile_src(jax.random.fold_in(key_of[10], 71), 0),
        "tile_count": draw_tile_count(jax.random.fold_in(key_of[10], 71), 0),
        "send_rows": with_ends(jax.random.randint(key_of[7], (N_DOM, N_DOM, CAP), 0, ROWS_DEV), jax.random.fold_in(key_of[7], 1), 0, ROWS_DEV - 1).astype(jnp.int32),
        "send_count": draw_send_count(jax.random.fold_in(key_of[10], 71), 0),
        "hub_rows": with_ends(jax.random.randint(key_of[9], (N_DOM, HUB_DEV), 0, ROWS_DEV), jax.random.fold_in(key_of[9], 1), 0, ROWS_DEV - 1).astype(jnp.int32),
    }


def source_table(features, send_rows, send_count, hub_rows, part):
    senders = jnp.arange(N_DOM, dtype=jnp.int32)
    rows_in = lax.dynamic_index_in_dim(send_rows, part, 1, keepdims=False)
    counts_in = lax.dynamic_index_in_dim(send_count, part, 1, keepdims=False)
    slot_valid = jnp.arange(CAP, dtype=jnp.int32)[None, :] < counts_in[:, None]
    bnd_index = (senders[:, None] * ROWS_DEV + rows_in).reshape(-1).astype(jnp.int32)
    bnd_valid = slot_valid.reshape(-1).astype(jnp.float32)
    boundary = jnp.where(bnd_valid[:, None] > 0.5, features[bnd_index], jnp.zeros((), jnp.bfloat16))
    hub_index = (senders[:, None] * ROWS_DEV + hub_rows).reshape(-1).astype(jnp.int32)
    hubs = features[hub_index]
    own = lax.dynamic_slice_in_dim(features, part * ROWS_DEV, ROWS_DEV, 0)
    table = jnp.concatenate([own, boundary.astype(jnp.bfloat16), hubs], axis=0)
    valid = jnp.concatenate([jnp.ones((ROWS_DEV,), jnp.float32), bnd_valid, jnp.ones((HUB,), jnp.float32)])
    return table, valid, bnd_index, bnd_valid, hub_index


def dense_adjacency(tiles, tile_src, tile_count, part, valid):
    blocks_own = ROWS_DEV // TILE
    sources = (ROWS_DEV + BND_DEV + HUB) // TILE
    tiles_part = lax.dynamic_slice_in_dim(tiles, part * blocks_own, blocks_own, 0).astype(jnp.float32)
    src_part = lax.dynamic_slice_in_dim(tile_src, part * blocks_own, blocks_own, 0)
    count_part = lax.dynamic_slice_in_dim(tile_count, part * blocks_own, blocks_own, 0)
    active = (jnp.arange(TMAX, dtype=jnp.int32)[None, :] < count_part[:, None]).astype(jnp.float32)
    onehot = (src_part[:, :, None] == jnp.arange(sources, dtype=jnp.int32)[None, None, :]).astype(jnp.float32)
    onehot = onehot * active[:, :, None]
    adjacency = jnp.einsum("tks,tkij->tisj", onehot, tiles_part, precision=lax.Precision.HIGHEST)
    adjacency = adjacency.reshape(ROWS_DEV, sources * TILE)
    return adjacency * valid[None, :]


def reference(features, w_self, w_neigh, cotangent, tiles, tile_src, tile_count, send_rows, send_count, hub_rows):
    def forward_part(part):
        part = part.astype(jnp.int32)
        table, valid, bnd_index, bnd_valid, hub_index = source_table(features, send_rows, send_count, hub_rows, part)
        adjacency = dense_adjacency(tiles, tile_src, tile_count, part, valid)
        degree = jnp.sum(adjacency, axis=1)
        numer = jnp.dot(adjacency, table.astype(jnp.float32), precision=lax.Precision.HIGHEST)
        return (numer / degree[:, None]).astype(jnp.bfloat16), degree

    agg, degree = lax.map(forward_part, jnp.arange(N_DOM, dtype=jnp.int32))
    agg = agg.reshape(NODES, F)
    degree = degree.reshape(NODES)
    pre = jnp.dot(features, w_self, preferred_element_type=jnp.float32) + jnp.dot(agg, w_neigh, preferred_element_type=jnp.float32)
    sigmoid_pre = jax.nn.sigmoid(pre)
    layer_out = (pre * sigmoid_pre).astype(jnp.bfloat16)
    grad_pre = (cotangent.astype(jnp.float32) * sigmoid_pre * (1.0 + pre * (1.0 - sigmoid_pre))).astype(jnp.bfloat16)
    grad_w_self = jnp.dot(features.T, grad_pre, preferred_element_type=jnp.float32)
    grad_w_neigh = jnp.dot(agg.T, grad_pre, preferred_element_type=jnp.float32)
    grad_scaled = (jnp.dot(grad_pre, w_neigh.T, preferred_element_type=jnp.float32) / degree[:, None]).astype(jnp.bfloat16)
    grad_start = jnp.dot(grad_pre, w_self.T, preferred_element_type=jnp.float32)

    def backward_part(part, grad_features):
        part = part.astype(jnp.int32)
        table, valid, bnd_index, bnd_valid, hub_index = source_table(features, send_rows, send_count, hub_rows, part)
        adjacency = dense_adjacency(tiles, tile_src, tile_count, part, valid)
        scaled_part = lax.dynamic_slice_in_dim(grad_scaled, part * ROWS_DEV, ROWS_DEV, 0).astype(jnp.float32)
        grad_source = jnp.dot(adjacency.T, scaled_part, precision=lax.Precision.HIGHEST)
        own_rows = part * ROWS_DEV + jnp.arange(ROWS_DEV, dtype=jnp.int32)
        grad_features = grad_features.at[own_rows].add(grad_source[:ROWS_DEV])
        grad_features = grad_features.at[bnd_index].add(grad_source[ROWS_DEV:ROWS_DEV + BND_DEV] * bnd_valid[:, None])
        grad_features = grad_features.at[hub_index].add(grad_source[ROWS_DEV + BND_DEV:])
        return grad_features

    grad_features = lax.fori_loop(0, N_DOM, backward_part, grad_start)
    return layer_out, grad_features, grad_w_self, grad_w_neigh
```

```python
import functools

import jax
import jax.numpy as jnp
from jax import lax
from jax.experimental import pallas as pl
from jax.experimental.pallas import tpu as pltpu
from jax.sharding import PartitionSpec as P

BF16 = jnp.bfloat16
F32 = jnp.float32
LANES = 128
MIB = 1 << 20


def mm(a, b, contract=((1,), (0,))):
    return lax.dot_general(a, b, (contract, ((), ())), preferred_element_type=F32)


def params(mib):
    return pltpu.CompilerParams(vmem_limit_bytes=mib * MIB)


def cost(flops, moved):
    return pl.CostEstimate(flops=flops, bytes_accessed=moved, transcendentals=0)


def pack_kernel(caps, idx_ref, feat_ref, out_ref):
    parts, _, _ = out_ref.shape
    bnd = parts * caps
    idx = idx_ref[...]
    rows = feat_ref.shape[0]
    hit = lax.broadcasted_iota(jnp.int32, (idx.shape[0], rows), 1) == idx
    picked = mm(jnp.where(hit, 1.0, 0.0).astype(BF16), feat_ref[...])
    picked = jnp.where(idx >= 0, picked, jnp.inf)
    groups = picked.shape[1] // LANES
    sub = lax.broadcasted_iota(jnp.int32, (8, LANES), 0)
    hubs = []
    for g in range(groups):
        piece = picked[:bnd, g * LANES : (g + 1) * LANES].astype(BF16)
        out_ref[:, g * caps : (g + 1) * caps, :] = piece.reshape(parts, caps, LANES)
        hubs.append(picked[bnd : bnd + 8, g * LANES : (g + 1) * LANES])
    rows_hub = [jnp.where(sub < 4, hubs[2 * j], hubs[2 * j + 1]) for j in range(groups // 2)]
    block = jnp.concatenate(rows_hub, axis=0).astype(BF16)
    out_ref[:, groups * caps :, :] = jnp.broadcast_to(block[None], (parts, groups * 4, LANES))


def early_kernel(src_ref, count_ref, tiles_ref, feat_ref, rows_ref, w_ref, *rest):
    own_ref, bnd_ref, own_t_ref, bnd_t_ref, numer_ref, degree_ref, pre_ref, acc = rest
    step = pl.program_id(0)
    here, slots, tile, _ = tiles_ref.shape
    own = own_ref.shape[1]
    acc[...] = jnp.zeros_like(acc)
    for t in range(here):
        block = step * here + t
        for k in range(slots):

            @pl.when(k < count_ref[block])
            def _():
                at = pl.ds(pl.multiple_of(src_ref[block, k] * tile, tile), tile)
                acc[t * tile : (t + 1) * tile, at] += tiles_ref[t, k].astype(F32)

    dense = acc[...].astype(BF16)
    own_ref[...] = dense[:, :own]
    bnd_ref[...] = dense[:, own:]
    flipped = dense.T
    own_t_ref[...] = flipped[:own]
    bnd_t_ref[...] = flipped[own:]
    numer_ref[...] = mm(dense[:, :own], feat_ref[...])
    degree_ref[...] = mm(dense[:, :own], jnp.ones((own, LANES), BF16))
    pre_ref[...] = mm(rows_ref[...], w_ref[...])


def unpack_table(caps, got_ref, table):
    parts = got_ref.shape[0]
    bnd = parts * caps
    width = table.shape[1] - LANES
    groups = width // LANES
    for g in range(groups):
        piece = got_ref[:, g * caps : (g + 1) * caps, :].astype(F32).reshape(bnd, LANES)
        used = piece < jnp.inf
        table[:bnd, g * LANES : (g + 1) * LANES] = jnp.where(used, piece, 0.0).astype(BF16)
        if g == 0:
            table[:bnd, width:] = jnp.where(used, 1.0, 0.0).astype(BF16)
    hub_rows = groups * 4
    hubs = got_ref[:, groups * caps :, :].astype(F32).reshape(parts * hub_rows, LANES)
    down = pltpu.roll(hubs, 4, 0).reshape(parts // 2, 2 * hub_rows, LANES)
    up = pltpu.roll(hubs, parts * hub_rows - 4, 0).reshape(parts // 2, 2 * hub_rows, LANES)
    hubs = hubs.reshape(parts // 2, 2 * hub_rows, LANES)
    low = lax.broadcasted_iota(jnp.int32, (parts // 2, hub_rows, LANES), 1) % 8 < 4
    even = jnp.where(low, hubs[:, :hub_rows], down[:, hub_rows:]).astype(BF16)
    odd = jnp.where(low, up[:, :hub_rows], hubs[:, hub_rows:]).astype(BF16)
    for g in range(groups):
        half = even if g % 2 == 0 else odd
        j = g // 2
        piece = half[:, 8 * j : 8 * j + 8, :].reshape(parts * 4, LANES)
        table[bnd:, g * LANES : (g + 1) * LANES] = piece
    table[bnd:, width:] = jnp.ones((parts * 4, LANES), BF16)


def main_kernel(caps, got_ref, bnd_ref, numer_ref, degree_ref, pre_ref, w_ref, cot_ref, *rest):
    out_ref, gp_ref, agg_ref, inv_ref, table = rest

    @pl.when(pl.program_id(0) == 0)
    def _():
        unpack_table(caps, got_ref, table)

    width = numer_ref.shape[1]
    adj = bnd_ref[...]
    numer = numer_ref[...] + mm(adj, table[:, :width])
    inv = 1.0 / (degree_ref[...] + mm(adj, table[:, width:]))
    inv_ref[...] = inv
    agg = (numer * jnp.concatenate([inv] * (width // LANES), axis=1)).astype(BF16)
    agg_ref[...] = agg
    pre = pre_ref[...] + mm(agg, w_ref[...])
    sig = jax.nn.sigmoid(pre)
    out_ref[...] = (pre * sig).astype(BF16)
    gp_ref[...] = (cot_ref[...].astype(F32) * sig * (1.0 + pre * (1.0 - sig))).astype(BF16)


def weight_kernel(masks, x_ref, gp_ref, keep_ref, send_ref, acc):
    me = lax.axis_index("dom")
    acc[...] = mm(x_ref[...], gp_ref[...], ((0,), (0,)))
    share = keep_ref.shape[1]
    for p, mask in enumerate(masks):
        mine = jnp.bitwise_xor(me, mask)
        other = jnp.bitwise_xor(me, mask + 1)
        keep_ref[p] = acc[pl.ds(pl.multiple_of(mine * share, 8), share), :]
        send_ref[p] = acc[pl.ds(pl.multiple_of(other * share, 8), share), :].astype(BF16)


def back_kernel(caps, gp_ref, w_ref, inv_ref, bnd_t_ref, gs_ref, out_ref):
    parts = out_ref.shape[0]
    bnd = parts * caps
    width = gs_ref.shape[1]
    groups = width // LANES
    inv = inv_ref[...]
    scaled = mm(gp_ref[...], w_ref[...], ((1,), (1,)))
    gs = (scaled * jnp.concatenate([inv] * groups, axis=1)).astype(BF16)
    gs_ref[...] = gs
    grads = mm(bnd_t_ref[...], gs)
    for g in range(groups):
        piece = grads[:bnd, g * LANES : (g + 1) * LANES].astype(BF16)
        out_ref[:, g * caps : (g + 1) * caps, :] = piece.reshape(parts, caps, LANES)
    half = parts // 2
    low = lax.broadcasted_iota(jnp.int32, (half, 8, LANES), 1) < 4
    even, odd = [], []
    for j in range(groups // 2):
        a = grads[bnd:, 2 * j * LANES : (2 * j + 1) * LANES]
        b = grads[bnd:, (2 * j + 1) * LANES : (2 * j + 2) * LANES]
        up = pltpu.roll(a, parts * 4 - 4, 0).reshape(half, 8, LANES)
        down = pltpu.roll(b, 4, 0).reshape(half, 8, LANES)
        a, b = a.reshape(half, 8, LANES), b.reshape(half, 8, LANES)
        even.append(jnp.where(low, a, down))
        odd.append(jnp.where(low, up, b))
    even = jnp.concatenate(even, axis=1)
    odd = jnp.concatenate(odd, axis=1)
    hubs = jnp.concatenate([even, odd], axis=1).reshape(parts, groups * 4, LANES)
    out_ref[:, groups * caps :, :] = hubs.astype(BF16)


def own_kernel(gp_ref, w_ref, own_t_ref, gs_ref, out_ref):
    out_ref[...] = mm(gp_ref[...], w_ref[...], ((1,), (1,))) + mm(own_t_ref[...], gs_ref[...])


def final_kernel(caps, hub_ref, own_ref, got_ref, idx_ref, out_ref, rows):
    parts = got_ref.shape[0]
    bnd = parts * caps
    width = out_ref.shape[1]
    groups = width // LANES
    for g in range(groups):
        piece = got_ref[:, g * caps : (g + 1) * caps, :]
        rows[:, g * LANES : (g + 1) * LANES] = piece.reshape(bnd, LANES)
    hit = lax.broadcasted_iota(jnp.int32, (out_ref.shape[0], bnd), 0) == idx_ref[...]
    out_ref[...] = own_ref[...] + mm(jnp.where(hit, 1.0, 0.0).astype(BF16), rows[...])
    hubs = jnp.sum(got_ref[:, groups * caps :, :].astype(F32), axis=0)
    for i in range(4):
        row = jnp.concatenate([hubs[4 * g + i : 4 * g + i + 1] for g in range(groups)], axis=1)
        out_ref[pl.ds(hub_ref[0, i], 1), :] += row


def swap(x, mask, parts):
    return lax.ppermute(x, "dom", [(d, d ^ mask) for d in range(parts)])


VMEM = pl.BlockSpec(memory_space=pltpu.VMEM)
SMEM = pl.BlockSpec(memory_space=pltpu.SMEM)


def on_device_fast(
    features,
    w_self,
    w_neigh,
    cotangent,
    tiles,
    tile_src,
    tile_count,
    send_rows,
    send_count,
    hub_rows,
):
    parts = lax.axis_size("dom")
    rows, width = features.shape
    hidden = w_self.shape[1]
    blocks, slots, tile, _ = tiles.shape
    caps = send_rows.shape[2]
    hub_own = hub_rows.shape[1]
    bnd = parts * caps
    far = bnd + parts * hub_own
    groups = width // LANES
    sent_rows = groups * (caps + hub_own)
    shape = jax.ShapeDtypeStruct

    used = jnp.arange(caps, dtype=jnp.int32)[None, :] < send_count[0][:, None]
    idx = jnp.where(used, send_rows[0], -1)
    idx_col = jnp.concatenate([idx.reshape(bnd), hub_rows[0], hub_rows[0], hub_rows[0], hub_rows[0]])
    idx_col = idx_col.reshape(bnd + 16, 1)
    idx_row = idx.reshape(1, bnd)

    outgoing = pl.pallas_call(
        functools.partial(pack_kernel, caps),
        out_shape=shape((parts, sent_rows, LANES), BF16),
        in_specs=[VMEM, VMEM],
        out_specs=VMEM,
        compiler_params=params(24),
        cost_estimate=cost(2 * bnd * rows * width, 4 * MIB),
        name="pack",
    )(idx_col, features)
    got = lax.all_to_all(outgoing, "dom", split_axis=0, concat_axis=0, tiled=True)

    steps = 4
    per = rows // steps
    row_block = lambda n: pl.BlockSpec((per, n), lambda s: (s, 0))
    col_block = lambda n: pl.BlockSpec((n, per), lambda s: (0, s))
    whole = lambda *n: pl.BlockSpec(n, lambda s: (0,) * len(n))
    own_adj, bnd_adj, own_adj_t, bnd_adj_t, numer, degree, pre_self = pl.pallas_call(
        early_kernel,
        grid=(steps,),
        out_shape=(
            shape((rows, rows), BF16),
            shape((rows, far), BF16),
            shape((rows, rows), BF16),
            shape((far, rows), BF16),
            shape((rows, width), F32),
            shape((rows, LANES), F32),
            shape((rows, hidden), F32),
        ),
        in_specs=[
            SMEM,
            SMEM,
            pl.BlockSpec((blocks // steps, slots, tile, tile), lambda s: (s, 0, 0, 0)),
            whole(rows, width),
            row_block(width),
            whole(width, hidden),
        ],
        out_specs=(
            row_block(rows),
            row_block(far),
            col_block(rows),
            col_block(far),
            row_block(width),
            row_block(LANES),
            row_block(hidden),
        ),
        scratch_shapes=[pltpu.VMEM((per, rows + far), F32)],
        compiler_params=params(32),
        cost_estimate=cost(6 * 10**9, 16 * MIB),
        name="early",
    )(tile_src, tile_count, tiles, features, features, w_self)

    layer_out, grad_pre, agg, inv = pl.pallas_call(
        functools.partial(main_kernel, caps),
        grid=(steps,),
        out_shape=(
            shape((rows, hidden), BF16),
            shape((rows, hidden), BF16),
            shape((rows, width), BF16),
            shape((rows, LANES), F32),
        ),
        in_specs=[
            whole(parts, sent_rows, LANES),
            row_block(far),
            row_block(width),
            row_block(LANES),
            row_block(hidden),
            whole(width, hidden),
            row_block(hidden),
        ],
        out_specs=(row_block(hidden), row_block(hidden), row_block(width), row_block(LANES)),
        scratch_shapes=[pltpu.VMEM((far, width + LANES), BF16)],
        compiler_params=params(32),
        cost_estimate=cost(4 * 10**9, 16 * MIB),
        name="middle",
    )(got, bnd_adj, numer, degree, pre_self, w_neigh, cotangent)

    share = width // parts
    half = parts // 2

    def weight_partial(x, first, second, name):
        masks = [first * (p >> 3) | second * (p >> 2 & 1) | (p & 3) << 3 for p in range(half)]
        return pl.pallas_call(
            functools.partial(weight_kernel, masks),
            out_shape=(shape((half, share, hidden), F32), shape((half, share, hidden), BF16)),
            in_specs=[VMEM, VMEM],
            out_specs=(VMEM, VMEM),
            scratch_shapes=[pltpu.VMEM((width, hidden), F32)],
            compiler_params=params(32),
            cost_estimate=cost(2 * rows * width * hidden, 10 * MIB),
            name=name,
        )(x, grad_pre)

    def plane_sum(keep, send, first, second):
        total = keep + swap(send, 1, parts).astype(F32)
        total = total[:8] + swap(total[8:].astype(BF16), first, parts).astype(F32)
        return total[:4] + swap(total[4:].astype(BF16), second, parts).astype(F32)

    keep_s, send_s = weight_partial(features, 2, 4, "weight_self")
    keep_n, send_n = weight_partial(agg, 4, 2, "weight_neigh")
    plane = jnp.stack([plane_sum(keep_s, send_s, 2, 4), plane_sum(keep_n, send_n, 4, 2)])
    total = plane[:, 0]
    for far_z in range(1, 4):
        total = total + swap(plane[:, far_z].astype(BF16), far_z << 3, parts).astype(F32)

    gs, back = pl.pallas_call(
        functools.partial(back_kernel, caps),
        out_shape=(shape((rows, width), BF16), shape((parts, sent_rows, LANES), BF16)),
        in_specs=[VMEM] * 4,
        out_specs=(VMEM, VMEM),
        compiler_params=params(32),
        cost_estimate=cost(3 * 10**9, 8 * MIB),
        name="back",
    )(grad_pre, w_neigh, inv, bnd_adj_t)
    returned = lax.all_to_all(back, "dom", split_axis=0, concat_axis=0, tiled=True)

    own_grad = pl.pallas_call(
        own_kernel,
        out_shape=shape((rows, width), F32),
        in_specs=[VMEM] * 4,
        out_specs=VMEM,
        compiler_params=params(32),
        cost_estimate=cost(3 * 10**9, 10 * MIB),
        name="own",
    )(grad_pre, w_self, own_adj_t, gs)

    grad_features = pl.pallas_call(
        functools.partial(final_kernel, caps),
        out_shape=shape((rows, width), F32),
        in_specs=[SMEM, VMEM, VMEM, VMEM],
        out_specs=VMEM,
        scratch_shapes=[pltpu.VMEM((bnd, width), BF16)],
        compiler_params=params(32),
        cost_estimate=cost(10**9, 8 * MIB),
        name="final",
    )(hub_rows, own_grad, returned, idx_row)
    return layer_out, grad_features, total[0], total[1]


def on_device(
    features,
    w_self,
    w_neigh,
    cotangent,
    tiles,
    tile_src,
    tile_count,
    send_rows,
    send_count,
    hub_rows,
):
    groups = lax.axis_size("dom")
    position = lax.axis_index("dom")
    own_rows, width = features.shape
    blocks_own, slots, tile_rows, _ = tiles.shape
    cap_rows = send_rows.shape[2]
    hub_own = hub_rows.shape[1]
    bnd_rows = groups * cap_rows
    hub_total = groups * hub_own
    sources = (own_rows + bnd_rows + hub_total) // tile_rows
    rows_out = send_rows[0]
    counts_out = send_count[0]
    slot_range = jnp.arange(cap_rows, dtype=jnp.int32)
    out_valid = slot_range[None, :] < counts_out[:, None]
    outgoing = jnp.where(out_valid[:, :, None], features[rows_out], jnp.zeros((), jnp.bfloat16))
    boundary, counts_in = (
        lax.all_to_all(outgoing, "dom", split_axis=0, concat_axis=0, tiled=True),
        lax.all_to_all(counts_out[:, None], "dom", split_axis=0, concat_axis=0, tiled=True),
    )
    in_valid = (slot_range[None, :] < counts_in).astype(jnp.float32).reshape(bnd_rows)
    boundary = boundary.reshape(bnd_rows, width)
    hub_mine = features[hub_rows[0]]
    hub_table = lax.all_gather(hub_mine, "dom", axis=0, tiled=True)
    table = jnp.concatenate([features, boundary, hub_table], axis=0)
    valid = jnp.concatenate(
        [jnp.ones((own_rows,), jnp.float32), in_valid, jnp.ones((hub_total,), jnp.float32)]
    )
    table_blocks = table.reshape(sources, tile_rows, width)
    valid_blocks = valid.reshape(sources, tile_rows)
    active = (jnp.arange(slots, dtype=jnp.int32)[None, :] < tile_count[:, None]).astype(jnp.float32)
    column_mask = valid_blocks[tile_src] * active[:, :, None]
    masked = tiles * column_mask[:, :, None, :].astype(jnp.bfloat16)
    picked = table_blocks[tile_src]
    numer = jnp.einsum("tkij,tkjf->tif", masked, picked, preferred_element_type=jnp.float32)
    degree = jnp.sum(masked, axis=(1, 3), dtype=jnp.float32).reshape(own_rows)
    agg = (numer.reshape(own_rows, width) / degree[:, None]).astype(jnp.bfloat16)
    pre = jnp.dot(features, w_self, preferred_element_type=jnp.float32) + jnp.dot(
        agg, w_neigh, preferred_element_type=jnp.float32
    )
    sigmoid_pre = jax.nn.sigmoid(pre)
    layer_out = (pre * sigmoid_pre).astype(jnp.bfloat16)
    grad_pre = (
        cotangent.astype(jnp.float32) * sigmoid_pre * (1.0 + pre * (1.0 - sigmoid_pre))
    ).astype(jnp.bfloat16)
    self_local = jnp.dot(features.T, grad_pre, preferred_element_type=jnp.float32)
    neigh_local = jnp.dot(agg.T, grad_pre, preferred_element_type=jnp.float32)
    self_total, neigh_total = lax.psum((self_local, neigh_local), "dom")
    share = width // groups
    grad_w_self = lax.dynamic_slice_in_dim(self_total, position * share, share, 0)
    grad_w_neigh = lax.dynamic_slice_in_dim(neigh_total, position * share, share, 0)
    grad_scaled = (
        jnp.dot(grad_pre, w_neigh.T, preferred_element_type=jnp.float32) / degree[:, None]
    ).astype(jnp.bfloat16)
    grad_scaled = grad_scaled.reshape(blocks_own, tile_rows, width)
    back_terms = jnp.einsum(
        "tkij,tif->tkjf", masked, grad_scaled, preferred_element_type=jnp.float32
    )
    placement = (
        tile_src[:, :, None] == jnp.arange(sources, dtype=jnp.int32)[None, None, :]
    ).astype(jnp.float32)
    grad_source = jnp.einsum(
        "tks,tkjf->sjf", placement, back_terms, precision=lax.Precision.HIGHEST
    )
    grad_source = grad_source.reshape(sources * tile_rows, width)
    grad_features = (
        jnp.dot(grad_pre, w_self.T, preferred_element_type=jnp.float32) + grad_source[:own_rows]
    )
    bnd_grads = grad_source[own_rows : own_rows + bnd_rows].reshape(groups, cap_rows, width)
    returned = lax.all_to_all(
        bnd_grads.astype(jnp.bfloat16), "dom", split_axis=0, concat_axis=0, tiled=True
    ).astype(bnd_grads.dtype)
    returned = returned * out_valid[:, :, None].astype(jnp.float32)
    grad_features = grad_features.at[rows_out.reshape(-1)].add(returned.reshape(bnd_rows, width))
    hub_back = lax.psum_scatter(
        grad_source[own_rows + bnd_rows :], "dom", scatter_dimension=0, tiled=True
    )
    grad_features = grad_features.at[hub_rows[0]].add(hub_back)
    return (layer_out, grad_features, grad_w_self, grad_w_neigh)


def on_any_device(*args):
    features, send_rows, hub_rows = args[0], args[7], args[9]
    parts = lax.axis_size("dom")
    share = features.shape[1] // parts
    if parts == 32 and share % 8 == 0 and send_rows.shape[2] % 16 == 0 and hub_rows.shape[1] == 4:
        return on_device_fast(*args)
    return on_device(*args)


def solution(mesh):
    in_specs = (
        P("dom", None),
        P(),
        P(),
        P("dom", None),
        P("dom", None, None, None),
        P("dom", None),
        P("dom"),
        P("dom", None, None),
        P("dom", None),
        P("dom", None),
    )
    out_specs = (P("dom", None), P("dom", None), P("dom", None), P("dom", None))
    return jax.shard_map(
        on_any_device, mesh=mesh, in_specs=in_specs, out_specs=out_specs, check_vma=False
    )
```

```python
import functools

import jax
import jax.numpy as jnp
from jax import lax
from jax.experimental import pallas as pl
from jax.experimental.pallas import tpu as pltpu
from jax.sharding import PartitionSpec as P

BF16 = jnp.bfloat16
F32 = jnp.float32
LANES = 128
MIB = 1 << 20
LIMIT = 58


def mm(a, b, contract=((1,), (0,))):
    return lax.dot_general(a, b, (contract, ((), ())), preferred_element_type=F32)


def params(mib):
    return pltpu.CompilerParams(vmem_limit_bytes=mib * MIB)


def cost(flops, moved):
    return pl.CostEstimate(flops=flops, bytes_accessed=moved, transcendentals=0)


def slot_indices(send_ref, count_ref):
    sub = lax.broadcasted_iota(jnp.int32, send_ref.shape, 0)
    return jnp.where(sub < count_ref[...], send_ref[...], -1)


def pack_kernel(send_ref, count_ref, hub_ref, feat_ref, out_ref, hits):
    caps, parts = send_ref.shape
    rows, width = feat_ref.shape
    bnd = parts * caps
    groups = width // LANES
    idx = slot_indices(send_ref, count_ref)
    lane = lax.broadcasted_iota(jnp.int32, (caps, rows), 1)
    for d in range(parts):
        hit = jnp.where(lane == idx[:, d : d + 1], 1.0, 0.0)
        hits[d * caps : (d + 1) * caps, :] = hit.astype(BF16)
    sub = lax.broadcasted_iota(jnp.int32, (16, rows), 0) % 4
    lane = lax.broadcasted_iota(jnp.int32, (16, rows), 1)
    hub = jnp.zeros((16, rows), F32)
    for i in range(4):
        hub = jnp.where((sub == i) & (lane == hub_ref[0, i]), 1.0, hub)
    hits[bnd:, :] = hub.astype(BF16)
    picked = mm(hits[...], feat_ref[...])
    for d in range(parts):
        piece = picked[d * caps : (d + 1) * caps]
        piece = jnp.where(idx[:, d : d + 1] >= 0, piece, jnp.inf).astype(BF16)
        for g in range(groups):
            out_ref[d, g * caps : (g + 1) * caps, :] = piece[:, g * LANES : (g + 1) * LANES]
    hubs = picked[bnd : bnd + 8]
    low = lax.broadcasted_iota(jnp.int32, (8, LANES), 0) < 4
    block = []
    for j in range(groups // 2):
        left = hubs[:, 2 * j * LANES : (2 * j + 1) * LANES]
        right = hubs[:, (2 * j + 1) * LANES : (2 * j + 2) * LANES]
        block.append(jnp.where(low, left, right))
    block = jnp.concatenate(block, axis=0).astype(BF16)
    out_ref[:, groups * caps :, :] = jnp.broadcast_to(block[None], (parts, groups * 4, LANES))


def early_kernel(src_ref, count_ref, tiles_ref, feat_ref, *rest):
    bnd_ref, own_t_ref, numer_ref, degree_ref, acc = rest
    step = pl.program_id(0)
    here, slots, tile, _ = tiles_ref.shape
    own = own_t_ref.shape[0]
    acc[...] = jnp.zeros_like(acc)
    for t in range(here):
        block = step * here + t
        for k in range(slots):

            @pl.when(k < count_ref[block])
            def _():
                at = pl.ds(pl.multiple_of(src_ref[block, k] * tile, tile), tile)
                acc[t * tile : (t + 1) * tile, at] += tiles_ref[t, k].astype(F32)

    dense = acc[...].astype(BF16)
    bnd_ref[...] = dense[:, own:]
    own_t_ref[...] = dense[:, :own].T
    numer_ref[...] = mm(dense[:, :own], feat_ref[...])
    degree_ref[...] = mm(dense[:, :own], jnp.ones((own, LANES), BF16))


def unpack_table(caps, got_ref, table):
    parts = got_ref.shape[0]
    bnd = parts * caps
    width = table.shape[1] - LANES
    groups = width // LANES
    for g in range(groups):
        piece = got_ref[:, g * caps : (g + 1) * caps, :].astype(F32).reshape(bnd, LANES)
        used = piece < jnp.inf
        table[:bnd, g * LANES : (g + 1) * LANES] = jnp.where(used, piece, 0.0).astype(BF16)
        if g == 0:
            table[:bnd, width:] = jnp.where(used, 1.0, 0.0).astype(BF16)
    hub_rows = groups * 4
    hubs = got_ref[:, groups * caps :, :].astype(F32).reshape(parts * hub_rows, LANES)
    down = pltpu.roll(hubs, 4, 0).reshape(parts // 2, 2 * hub_rows, LANES)
    up = pltpu.roll(hubs, parts * hub_rows - 4, 0).reshape(parts // 2, 2 * hub_rows, LANES)
    hubs = hubs.reshape(parts // 2, 2 * hub_rows, LANES)
    low = lax.broadcasted_iota(jnp.int32, (parts // 2, hub_rows, LANES), 1) % 8 < 4
    even = jnp.where(low, hubs[:, :hub_rows], down[:, hub_rows:]).astype(BF16)
    odd = jnp.where(low, up[:, :hub_rows], hubs[:, hub_rows:]).astype(BF16)
    for g in range(groups):
        half = even if g % 2 == 0 else odd
        j = g // 2
        piece = half[:, 8 * j : 8 * j + 8, :].reshape(parts * 4, LANES)
        table[bnd:, g * LANES : (g + 1) * LANES] = piece
    table[bnd:, width:] = jnp.ones((parts * 4, LANES), BF16)


def pack_grads(caps, grads, out_ref):
    parts = out_ref.shape[0]
    bnd = parts * caps
    groups = grads.shape[1] // LANES
    for g in range(groups):
        piece = grads[:bnd, g * LANES : (g + 1) * LANES].astype(BF16)
        out_ref[:, g * caps : (g + 1) * caps, :] = piece.reshape(parts, caps, LANES)
    half = parts // 2
    low = lax.broadcasted_iota(jnp.int32, (half, 8, LANES), 1) < 4
    even, odd = [], []
    for j in range(groups // 2):
        a = grads[bnd:, 2 * j * LANES : (2 * j + 1) * LANES]
        b = grads[bnd:, (2 * j + 1) * LANES : (2 * j + 2) * LANES]
        up = pltpu.roll(a, parts * 4 - 4, 0).reshape(half, 8, LANES)
        down = pltpu.roll(b, 4, 0).reshape(half, 8, LANES)
        a, b = a.reshape(half, 8, LANES), b.reshape(half, 8, LANES)
        even.append(jnp.where(low, a, down))
        odd.append(jnp.where(low, up, b))
    hubs = jnp.concatenate(even + odd, axis=1).reshape(parts, groups * 4, LANES)
    out_ref[:, groups * caps :, :] = hubs.astype(BF16)


def main_kernel(caps, masks, *refs):
    outs_hbm, held, outs_all = refs[8:16], refs[16:24], refs[24:32]
    table, pre_all, agg_all, acc, in_sem, out_sem, chain_sem, back_sem = refs[32:]
    out_hbm, gp_hbm, gs_hbm, *chain_hbm, back_hbm = outs_hbm
    out_all, gp_all, gs_all, *chain_all, back_all = outs_all
    got, bnd, numer, degree, feat, cot, wn, ws = held
    width = numer.shape[1]
    loads = [
        pltpu.make_async_copy(a, b, in_sem.at[i]) for i, (a, b) in enumerate(zip(refs[:8], held))
    ]
    for i in (7, 4, 0, 1, 3, 2, 6, 5):
        loads[i].start()
    for i in (7, 4):
        loads[i].wait()
    pre_all[...] = mm(feat[...], ws[...])
    loads[0].wait()
    unpack_table(caps, got, table)
    for i in (1, 2, 3):
        loads[i].wait()
    num = numer[...] + mm(bnd[...], table[:, :width])
    inv = 1.0 / (degree[...] + mm(bnd[...], table[:, width:]))
    degree[...] = inv
    agg = (num * jnp.concatenate([inv] * (width // LANES), axis=1)).astype(BF16)
    agg_all[...] = agg
    loads[6].wait()
    pre = pre_all[...] + mm(agg_all[...], wn[...])
    loads[5].wait()
    sig = 0.5 * jnp.tanh(0.5 * pre) + 0.5
    out = pre * sig
    out_all[...] = out.astype(BF16)
    gp_all[...] = (cot[...].astype(F32) * (sig + out * (1.0 - sig))).astype(BF16)
    stores = [pltpu.make_async_copy(out_all, out_hbm, out_sem.at[0])]
    stores.append(pltpu.make_async_copy(gp_all, gp_hbm, out_sem.at[1]))
    for store in stores:
        store.start()
    inv = jnp.concatenate([degree[...]] * (width // LANES), axis=1)
    gs_all[...] = (mm(gp_all[...], wn[...], ((1,), (1,))) * inv).astype(BF16)
    stores.append(pltpu.make_async_copy(gs_all, gs_hbm, out_sem.at[2]))
    stores[-1].start()
    me = lax.axis_index("dom")
    *keeps, send = chain_all
    share = send.shape[2]
    places = [(ref, p) for ref in keeps for p in range(ref.shape[1])]
    for chain, x in enumerate((agg_all, feat)):
        acc[...] = mm(x[...], gp_all[...], ((0,), (0,)))
        for p, mask in enumerate(masks[chain]):
            mine = jnp.bitwise_xor(me, mask)
            other = jnp.bitwise_xor(me, mask + 1)
            keep, at = places[p]
            keep[chain, at] = acc[pl.ds(pl.multiple_of(mine * share, 8), share), :]
            send[chain, p] = acc[pl.ds(pl.multiple_of(other * share, 8), share), :].astype(BF16)
        for i, (a, b) in enumerate(zip(chain_all, chain_hbm)):
            stores.append(pltpu.make_async_copy(a.at[chain], b.at[chain], chain_sem.at[chain, i]))
            stores[-1].start()
    pack_grads(caps, mm(bnd[...], gs_all[...], ((0,), (0,))), back_all)
    stores.append(pltpu.make_async_copy(back_all, back_hbm, back_sem))
    stores[-1].start()
    for store in stores:
        store.wait()


def stage_one_kernel(keep_ref, core_ref, a_ref, b_ref, token_ref):
    token_ref[...] = jnp.zeros_like(token_ref)
    for chain, ref in ((0, a_ref), (1, b_ref)):
        ref[...] = (keep_ref[chain] + core_ref[chain].astype(F32)).astype(BF16)


def stage_two_kernel(keep_ref, core_ref, a1_ref, b1_ref, _, a_ref, b_ref):
    for chain, got, ref in ((0, a1_ref, a_ref), (1, b1_ref, b_ref)):
        total = keep_ref[chain] + core_ref[chain].astype(F32) + got[...].astype(F32)
        ref[...] = total.astype(BF16)


def stage_z_kernel(keep_ref, core_ref, a1_ref, b1_ref, a2_ref, b2_ref, token_ref, base_ref, *outs):
    token_ref[...] = jnp.zeros_like(token_ref)
    for chain, one, two in ((0, a1_ref, a2_ref), (1, b1_ref, b2_ref)):
        total = keep_ref[chain] + core_ref[chain].astype(F32)
        total = total + one[...].astype(F32) + two[...].astype(F32)
        base_ref[chain] = total[0]
        for z, ref in enumerate(outs):
            ref[chain] = total[z + 1].astype(BF16)


def stage_last_kernel(base_ref, z1_ref, z2_ref, z3_ref, _, neigh_ref, self_ref):
    for chain, ref in ((0, neigh_ref), (1, self_ref)):
        total = base_ref[chain] + z1_ref[chain].astype(F32)
        ref[...] = total + z2_ref[chain].astype(F32) + z3_ref[chain].astype(F32)


def own_kernel(send_ref, count_ref, gp_ref, w_ref, own_t_ref, gs_ref, _, out_ref, place_ref, token_ref, hits):
    token_ref[...] = jnp.zeros_like(token_ref)
    out_ref[...] = mm(gp_ref[...], w_ref[...], ((1,), (1,))) + mm(own_t_ref[...], gs_ref[...])
    caps, parts = send_ref.shape
    here = hits.shape[1]
    idx = slot_indices(send_ref, count_ref) - pl.program_id(0) * here
    lane = lax.broadcasted_iota(jnp.int32, (caps, here), 1)
    for d in range(parts):
        hit = jnp.where(lane == idx[:, d : d + 1], 1.0, 0.0)
        hits[d * caps : (d + 1) * caps, :] = hit.astype(BF16)
    place_ref[...] = hits[...].T


def final_kernel(caps, hub_ref, own_ref, got_ref, place_ref, _, out_ref, token_ref, rows):
    token_ref[...] = jnp.zeros_like(token_ref)
    step = pl.program_id(0)
    parts = got_ref.shape[0]
    bnd = parts * caps
    here, width = out_ref.shape
    groups = width // LANES

    @pl.when(step == 0)
    def _():
        for g in range(groups):
            piece = got_ref[:, g * caps : (g + 1) * caps, :]
            rows[:, g * LANES : (g + 1) * LANES] = piece.reshape(bnd, LANES)

    out_ref[...] = own_ref[...] + mm(place_ref[...], rows[...])
    hubs = jnp.sum(got_ref[:, groups * caps :, :].astype(F32), axis=0)
    for i in range(4):
        row = jnp.concatenate([hubs[4 * g + i : 4 * g + i + 1] for g in range(groups)], axis=1)
        at = hub_ref[0, i] - step * here

        @pl.when((at >= 0) & (at < here))
        def _():
            out_ref[pl.ds(at, 1), :] += row


def swap(x, mask, parts):
    return lax.ppermute(x, "dom", [(d, d ^ mask) for d in range(parts)])


VMEM = pl.BlockSpec(memory_space=pltpu.VMEM)
SMEM = pl.BlockSpec(memory_space=pltpu.SMEM)
ANY = pl.BlockSpec(memory_space=pl.ANY)


def on_device_fast(
    features,
    w_self,
    w_neigh,
    cotangent,
    tiles,
    tile_src,
    tile_count,
    send_rows,
    send_count,
    hub_rows,
):
    parts = lax.axis_size("dom")
    rows, width = features.shape
    hidden = w_self.shape[1]
    blocks, slots, tile, _ = tiles.shape
    caps = send_rows.shape[2]
    hub_own = hub_rows.shape[1]
    bnd = parts * caps
    far = bnd + parts * hub_own
    groups = width // LANES
    sent_rows = groups * (caps + hub_own)
    shape = jax.ShapeDtypeStruct

    send_t = send_rows[0].T

    outgoing = pl.pallas_call(
        pack_kernel,
        out_shape=shape((parts, sent_rows, LANES), BF16),
        in_specs=[VMEM, VMEM, SMEM, VMEM],
        out_specs=VMEM,
        scratch_shapes=[pltpu.VMEM((bnd + 16, rows), BF16)],
        compiler_params=params(LIMIT),
        cost_estimate=cost(2 * bnd * rows * width, 4 * MIB),
        name="pack",
    )(send_t, send_count, hub_rows, features)
    got = lax.all_to_all(outgoing, "dom", split_axis=0, concat_axis=0, tiled=True)

    steps = 4
    per = rows // steps
    row_block = lambda n: pl.BlockSpec((per, n), lambda s: (s, 0))
    col_block = lambda n: pl.BlockSpec((n, per), lambda s: (0, s))
    whole = lambda *n: pl.BlockSpec(n, lambda s: (0,) * len(n))
    bnd_adj, own_adj_t, numer, degree = pl.pallas_call(
        early_kernel,
        grid=(steps,),
        out_shape=(
            shape((rows, far), BF16),
            shape((rows, rows), BF16),
            shape((rows, width), F32),
            shape((rows, LANES), F32),
        ),
        in_specs=[
            SMEM,
            SMEM,
            pl.BlockSpec((blocks // steps, slots, tile, tile), lambda s: (s, 0, 0, 0)),
            whole(rows, width),
        ],
        out_specs=(row_block(far), col_block(rows), row_block(width), row_block(LANES)),
        scratch_shapes=[pltpu.VMEM((per, rows + far), F32)],
        compiler_params=params(LIMIT),
        cost_estimate=cost(6 * 10**9, 16 * MIB),
        name="early",
    )(tile_src, tile_count, tiles, features)

    share = width // parts
    half = parts // 2
    order = lambda first, second: [
        first * (p >> 3) | second * (p >> 2 & 1) | (p & 3) << 3 for p in range(half)
    ]
    outs = [
        shape((rows, hidden), BF16),
        shape((rows, hidden), BF16),
        shape((rows, width), BF16),
        shape((2, 4, share, hidden), F32),
        shape((2, 4, share, hidden), F32),
        shape((2, 8, share, hidden), F32),
        shape((2, half, share, hidden), BF16),
        shape((parts, sent_rows, LANES), BF16),
    ]
    operands = [got, bnd_adj, numer, degree, features, cotangent, w_neigh, w_self]
    layer_out, grad_pre, gs, keep_low, keep_mid, keep_high, send, back = pl.pallas_call(
        functools.partial(main_kernel, caps, (order(4, 2), order(2, 4))),
        out_shape=tuple(outs),
        in_specs=[ANY] + [ANY] * 7,
        out_specs=(ANY,) * 8,
        scratch_shapes=[pltpu.VMEM(a.shape, a.dtype) for a in operands + outs]
        + [
            pltpu.VMEM((far, width + LANES), BF16),
            pltpu.VMEM((rows, hidden), F32),
            pltpu.VMEM((rows, width), BF16),
            pltpu.VMEM((width, hidden), F32),
            pltpu.SemaphoreType.DMA((8,)),
            pltpu.SemaphoreType.DMA((3,)),
            pltpu.SemaphoreType.DMA((2, 4)),
            pltpu.SemaphoreType.DMA(()),
        ],
        compiler_params=params(LIMIT),
        cost_estimate=cost(10**10, 24 * MIB),
        name="middle",
    )(*operands)

    core = swap(send, 1, parts)
    returned = lax.all_to_all(back, "dom", split_axis=0, concat_axis=0, tiled=True)

    both = lambda n, at: pl.BlockSpec((2, n, share, hidden), lambda s: (0, at, 0, 0))
    one = lambda n, at: pl.BlockSpec((n, share, hidden), lambda s: (at, 0, 0))

    def stage(kernel, name, in_specs, out_shape, out_specs, *operands):
        return pl.pallas_call(
            kernel,
            grid=(1,),
            out_shape=out_shape,
            in_specs=in_specs,
            out_specs=out_specs,
            compiler_params=params(12),
            cost_estimate=cost(10**6, 3 * MIB),
            name=name,
        )(*operands)

    halves = shape((half // 2, share, hidden), BF16)
    token = shape((8, LANES), F32)
    token_at = pl.BlockSpec((8, LANES), lambda s: (0, 0))
    a1, b1, sent_one = stage(
        stage_one_kernel,
        "stage_one",
        [both(8, 0), both(8, 1)],
        (halves, halves, token),
        (one(8, 0), one(8, 0), token_at),
        keep_high,
        core,
    )
    got_a1, got_b1 = swap(a1, 4, parts), swap(b1, 2, parts)
    own_grad, place, own_done = pl.pallas_call(
        own_kernel,
        grid=(steps,),
        out_shape=(shape((rows, width), F32), shape((rows, bnd), BF16), token),
        in_specs=[
            VMEM,
            VMEM,
            row_block(hidden),
            whole(width, hidden),
            row_block(rows),
            whole(rows, width),
            ANY,
        ],
        out_specs=(row_block(width), row_block(bnd), token_at),
        scratch_shapes=[pltpu.VMEM((bnd, per), BF16)],
        compiler_params=params(LIMIT),
        cost_estimate=cost(4 * 10**9, 10 * MIB),
        name="own",
    )(send_t, send_count, grad_pre, w_self, own_adj_t, gs, sent_one)

    quarters = shape((half // 4, share, hidden), BF16)
    a2, b2 = stage(
        stage_two_kernel,
        "stage_two",
        [both(4, 0), both(4, 1), one(4, 1), one(4, 1), ANY],
        (quarters, quarters),
        (one(4, 0), one(4, 0)),
        keep_mid,
        core,
        got_a1,
        got_b1,
        own_done,
    )
    got_a2, got_b2 = swap(a2, 2, parts), swap(b2, 4, parts)
    pair = shape((2, share, hidden), BF16)
    sent_z, base, *sends = stage(
        stage_z_kernel,
        "stage_z",
        [both(4, 0), both(4, 0), one(4, 0), one(4, 0), one(4, 0), one(4, 0)],
        (token, shape((2, share, hidden), F32), pair, pair, pair),
        (token_at,) + (one(2, 0),) * 4,
        keep_low,
        core,
        got_a1,
        got_b1,
        got_a2,
        got_b2,
    )
    got_z = [swap(x, z << 3, parts) for z, x in enumerate(sends, 1)]

    grad_features, final_done = pl.pallas_call(
        functools.partial(final_kernel, caps),
        grid=(steps,),
        out_shape=(shape((rows, width), F32), token),
        in_specs=[SMEM, row_block(width), whole(parts, sent_rows, LANES), row_block(bnd), ANY],
        out_specs=(row_block(width), token_at),
        scratch_shapes=[pltpu.VMEM((bnd, width), BF16)],
        compiler_params=params(LIMIT),
        cost_estimate=cost(10**9, 8 * MIB),
        name="final",
    )(hub_rows, own_grad, returned, place, sent_z)

    total = shape((share, hidden), F32)
    flat = pl.BlockSpec((share, hidden), lambda s: (0, 0))
    grad_neigh, grad_self = stage(
        stage_last_kernel,
        "stage_last",
        [one(2, 0)] * 4 + [ANY],
        (total, total),
        (flat, flat),
        base,
        *got_z,
        final_done,
    )
    return layer_out, grad_features, grad_self, grad_neigh


def on_device(
    features,
    w_self,
    w_neigh,
    cotangent,
    tiles,
    tile_src,
    tile_count,
    send_rows,
    send_count,
    hub_rows,
):
    groups = lax.axis_size("dom")
    position = lax.axis_index("dom")
    own_rows, width = features.shape
    blocks_own, slots, tile_rows, _ = tiles.shape
    cap_rows = send_rows.shape[2]
    hub_own = hub_rows.shape[1]
    bnd_rows = groups * cap_rows
    hub_total = groups * hub_own
    sources = (own_rows + bnd_rows + hub_total) // tile_rows
    rows_out = send_rows[0]
    counts_out = send_count[0]
    slot_range = jnp.arange(cap_rows, dtype=jnp.int32)
    out_valid = slot_range[None, :] < counts_out[:, None]
    outgoing = jnp.where(out_valid[:, :, None], features[rows_out], jnp.zeros((), jnp.bfloat16))
    boundary, counts_in = (
        lax.all_to_all(outgoing, "dom", split_axis=0, concat_axis=0, tiled=True),
        lax.all_to_all(counts_out[:, None], "dom", split_axis=0, concat_axis=0, tiled=True),
    )
    in_valid = (slot_range[None, :] < counts_in).astype(jnp.float32).reshape(bnd_rows)
    boundary = boundary.reshape(bnd_rows, width)
    hub_mine = features[hub_rows[0]]
    hub_table = lax.all_gather(hub_mine, "dom", axis=0, tiled=True)
    table = jnp.concatenate([features, boundary, hub_table], axis=0)
    valid = jnp.concatenate(
        [jnp.ones((own_rows,), jnp.float32), in_valid, jnp.ones((hub_total,), jnp.float32)]
    )
    table_blocks = table.reshape(sources, tile_rows, width)
    valid_blocks = valid.reshape(sources, tile_rows)
    active = (jnp.arange(slots, dtype=jnp.int32)[None, :] < tile_count[:, None]).astype(jnp.float32)
    column_mask = valid_blocks[tile_src] * active[:, :, None]
    masked = tiles * column_mask[:, :, None, :].astype(jnp.bfloat16)
    picked = table_blocks[tile_src]
    numer = jnp.einsum("tkij,tkjf->tif", masked, picked, preferred_element_type=jnp.float32)
    degree = jnp.sum(masked, axis=(1, 3), dtype=jnp.float32).reshape(own_rows)
    agg = (numer.reshape(own_rows, width) / degree[:, None]).astype(jnp.bfloat16)
    pre = jnp.dot(features, w_self, preferred_element_type=jnp.float32) + jnp.dot(
        agg, w_neigh, preferred_element_type=jnp.float32
    )
    sigmoid_pre = jax.nn.sigmoid(pre)
    layer_out = (pre * sigmoid_pre).astype(jnp.bfloat16)
    grad_pre = (
        cotangent.astype(jnp.float32) * sigmoid_pre * (1.0 + pre * (1.0 - sigmoid_pre))
    ).astype(jnp.bfloat16)
    self_local = jnp.dot(features.T, grad_pre, preferred_element_type=jnp.float32)
    neigh_local = jnp.dot(agg.T, grad_pre, preferred_element_type=jnp.float32)
    self_total, neigh_total = lax.psum((self_local, neigh_local), "dom")
    share = width // groups
    grad_w_self = lax.dynamic_slice_in_dim(self_total, position * share, share, 0)
    grad_w_neigh = lax.dynamic_slice_in_dim(neigh_total, position * share, share, 0)
    grad_scaled = (
        jnp.dot(grad_pre, w_neigh.T, preferred_element_type=jnp.float32) / degree[:, None]
    ).astype(jnp.bfloat16)
    grad_scaled = grad_scaled.reshape(blocks_own, tile_rows, width)
    back_terms = jnp.einsum(
        "tkij,tif->tkjf", masked, grad_scaled, preferred_element_type=jnp.float32
    )
    placement = (
        tile_src[:, :, None] == jnp.arange(sources, dtype=jnp.int32)[None, None, :]
    ).astype(jnp.float32)
    grad_source = jnp.einsum(
        "tks,tkjf->sjf", placement, back_terms, precision=lax.Precision.HIGHEST
    )
    grad_source = grad_source.reshape(sources * tile_rows, width)
    grad_features = (
        jnp.dot(grad_pre, w_self.T, preferred_element_type=jnp.float32) + grad_source[:own_rows]
    )
    bnd_grads = grad_source[own_rows : own_rows + bnd_rows].reshape(groups, cap_rows, width)
    returned = lax.all_to_all(
        bnd_grads.astype(jnp.bfloat16), "dom", split_axis=0, concat_axis=0, tiled=True
    ).astype(bnd_grads.dtype)
    returned = returned * out_valid[:, :, None].astype(jnp.float32)
    grad_features = grad_features.at[rows_out.reshape(-1)].add(returned.reshape(bnd_rows, width))
    hub_back = lax.psum_scatter(
        grad_source[own_rows + bnd_rows :], "dom", scatter_dimension=0, tiled=True
    )
    grad_features = grad_features.at[hub_rows[0]].add(hub_back)
    return (layer_out, grad_features, grad_w_self, grad_w_neigh)


def on_any_device(*args):
    features, send_rows, hub_rows = args[0], args[7], args[9]
    parts = lax.axis_size("dom")
    share = features.shape[1] // parts
    if parts == 32 and share % 8 == 0 and send_rows.shape[2] % 16 == 0 and hub_rows.shape[1] == 4:
        return on_device_fast(*args)
    return on_device(*args)


def solution(mesh):
    in_specs = (
        P("dom", None),
        P(),
        P(),
        P("dom", None),
        P("dom", None, None, None),
        P("dom", None),
        P("dom"),
        P("dom", None, None),
        P("dom", None),
        P("dom", None),
    )
    out_specs = (P("dom", None), P("dom", None), P("dom", None), P("dom", None))
    return jax.shard_map(
        on_any_device, mesh=mesh, in_specs=in_specs, out_specs=out_specs, check_vma=False
    )
```

```python
import functools

import jax
import jax.numpy as jnp
from jax import lax
from jax.experimental import pallas as pl
from jax.experimental.pallas import tpu as pltpu
from jax.sharding import PartitionSpec as P

BF16 = jnp.bfloat16
F32 = jnp.float32
LANES = 128
MIB = 1 << 20
LIMIT = 58


def mm(a, b, contract=((1,), (0,))):
    return lax.dot_general(a, b, (contract, ((), ())), preferred_element_type=F32)


def params(mib):
    return pltpu.CompilerParams(vmem_limit_bytes=mib * MIB)


def cost(flops, moved):
    return pl.CostEstimate(flops=flops, bytes_accessed=moved, transcendentals=0)


def slot_indices(send_ref, count_ref):
    sub = lax.broadcasted_iota(jnp.int32, send_ref.shape, 0)
    return jnp.where(sub < count_ref[...], send_ref[...], -1)


def pack_kernel(send_ref, count_ref, hub_ref, feat_ref, out_ref, hits):
    caps, parts = send_ref.shape
    rows, width = feat_ref.shape
    bnd = parts * caps
    groups = width // LANES
    idx = slot_indices(send_ref, count_ref)
    lane = lax.broadcasted_iota(jnp.int32, (caps, rows), 1)
    for d in range(parts):
        hit = jnp.where(lane == idx[:, d : d + 1], 1.0, 0.0)
        hits[d * caps : (d + 1) * caps, :] = hit.astype(BF16)
    sub = lax.broadcasted_iota(jnp.int32, (16, rows), 0) % 4
    lane = lax.broadcasted_iota(jnp.int32, (16, rows), 1)
    hub = jnp.zeros((16, rows), F32)
    for i in range(4):
        hub = jnp.where((sub == i) & (lane == hub_ref[0, i]), 1.0, hub)
    hits[bnd:, :] = hub.astype(BF16)
    picked = mm(hits[...], feat_ref[...])
    for d in range(parts):
        piece = picked[d * caps : (d + 1) * caps]
        piece = jnp.where(idx[:, d : d + 1] >= 0, piece, jnp.inf).astype(BF16)
        for g in range(groups):
            out_ref[d, g * caps : (g + 1) * caps, :] = piece[:, g * LANES : (g + 1) * LANES]
    hubs = picked[bnd : bnd + 8]
    low = lax.broadcasted_iota(jnp.int32, (8, LANES), 0) < 4
    block = []
    for j in range(groups // 2):
        left = hubs[:, 2 * j * LANES : (2 * j + 1) * LANES]
        right = hubs[:, (2 * j + 1) * LANES : (2 * j + 2) * LANES]
        block.append(jnp.where(low, left, right))
    block = jnp.concatenate(block, axis=0).astype(BF16)
    out_ref[:, groups * caps :, :] = jnp.broadcast_to(block[None], (parts, groups * 4, LANES))


def early_kernel(src_ref, count_ref, tiles_ref, feat_ref, *rest):
    bnd_ref, own_t_ref, numer_ref, degree_ref, acc = rest
    step = pl.program_id(0)
    here, slots, tile, _ = tiles_ref.shape
    own = own_t_ref.shape[0]
    acc[...] = jnp.zeros_like(acc)
    for t in range(here):
        block = step * here + t
        for k in range(slots):

            @pl.when(k < count_ref[block])
            def _():
                at = pl.ds(pl.multiple_of(src_ref[block, k] * tile, tile), tile)
                acc[t * tile : (t + 1) * tile, at] += tiles_ref[t, k].astype(F32)

    dense = acc[...].astype(BF16)
    bnd_ref[...] = dense[:, own:]
    own_t_ref[...] = dense[:, :own].T
    numer_ref[...] = mm(dense[:, :own], feat_ref[...])
    degree_ref[...] = mm(dense[:, :own], jnp.ones((own, LANES), BF16))


def unpack_table(caps, got_ref, table):
    parts = got_ref.shape[0]
    bnd = parts * caps
    width = table.shape[1] - LANES
    groups = width // LANES
    for g in range(groups):
        piece = got_ref[:, g * caps : (g + 1) * caps, :].astype(F32).reshape(bnd, LANES)
        used = piece < jnp.inf
        table[:bnd, g * LANES : (g + 1) * LANES] = jnp.where(used, piece, 0.0).astype(BF16)
        if g == 0:
            table[:bnd, width:] = jnp.where(used, 1.0, 0.0).astype(BF16)
    hub_rows = groups * 4
    hubs = got_ref[:, groups * caps :, :].astype(F32).reshape(parts * hub_rows, LANES)
    down = pltpu.roll(hubs, 4, 0).reshape(parts // 2, 2 * hub_rows, LANES)
    up = pltpu.roll(hubs, parts * hub_rows - 4, 0).reshape(parts // 2, 2 * hub_rows, LANES)
    hubs = hubs.reshape(parts // 2, 2 * hub_rows, LANES)
    low = lax.broadcasted_iota(jnp.int32, (parts // 2, hub_rows, LANES), 1) % 8 < 4
    even = jnp.where(low, hubs[:, :hub_rows], down[:, hub_rows:]).astype(BF16)
    odd = jnp.where(low, up[:, :hub_rows], hubs[:, hub_rows:]).astype(BF16)
    for g in range(groups):
        half = even if g % 2 == 0 else odd
        j = g // 2
        piece = half[:, 8 * j : 8 * j + 8, :].reshape(parts * 4, LANES)
        table[bnd:, g * LANES : (g + 1) * LANES] = piece
    table[bnd:, width:] = jnp.ones((parts * 4, LANES), BF16)


def pack_grads(caps, grads, out_ref):
    parts = out_ref.shape[0]
    bnd = parts * caps
    groups = grads.shape[1] // LANES
    for g in range(groups):
        piece = grads[:bnd, g * LANES : (g + 1) * LANES].astype(BF16)
        out_ref[:, g * caps : (g + 1) * caps, :] = piece.reshape(parts, caps, LANES)
    half = parts // 2
    low = lax.broadcasted_iota(jnp.int32, (half, 8, LANES), 1) < 4
    even, odd = [], []
    for j in range(groups // 2):
        a = grads[bnd:, 2 * j * LANES : (2 * j + 1) * LANES]
        b = grads[bnd:, (2 * j + 1) * LANES : (2 * j + 2) * LANES]
        up = pltpu.roll(a, parts * 4 - 4, 0).reshape(half, 8, LANES)
        down = pltpu.roll(b, 4, 0).reshape(half, 8, LANES)
        a, b = a.reshape(half, 8, LANES), b.reshape(half, 8, LANES)
        even.append(jnp.where(low, a, down))
        odd.append(jnp.where(low, up, b))
    hubs = jnp.concatenate(even + odd, axis=1).reshape(parts, groups * 4, LANES)
    out_ref[:, groups * caps :, :] = hubs.astype(BF16)


def main_kernel(caps, masks, *refs):
    outs_hbm, held, outs_all = refs[8:16], refs[16:24], refs[24:32]
    table, pre_all, agg_all, acc, in_sem, out_sem, chain_sem, back_sem = refs[32:]
    out_hbm, gp_hbm, gs_hbm, *chain_hbm, back_hbm = outs_hbm
    out_all, gp_all, gs_all, *chain_all, back_all = outs_all
    got, bnd, numer, degree, feat, cot, wn, ws = held
    width = numer.shape[1]
    loads = [
        pltpu.make_async_copy(a, b, in_sem.at[i]) for i, (a, b) in enumerate(zip(refs[:8], held))
    ]
    for i in (7, 4, 0, 1, 3, 2, 6, 5):
        loads[i].start()
    for i in (7, 4):
        loads[i].wait()
    pre_all[...] = mm(feat[...], ws[...])
    loads[0].wait()
    unpack_table(caps, got, table)
    for i in (1, 2, 3):
        loads[i].wait()
    num = numer[...] + mm(bnd[...], table[:, :width])
    inv = 1.0 / (degree[...] + mm(bnd[...], table[:, width:]))
    degree[...] = inv
    agg = (num * jnp.concatenate([inv] * (width // LANES), axis=1)).astype(BF16)
    agg_all[...] = agg
    loads[6].wait()
    pre = pre_all[...] + mm(agg_all[...], wn[...])
    loads[5].wait()
    sig = 0.5 * jnp.tanh(0.5 * pre) + 0.5
    out = pre * sig
    out_all[...] = out.astype(BF16)
    gp_all[...] = (cot[...].astype(F32) * (sig + out * (1.0 - sig))).astype(BF16)
    stores = [pltpu.make_async_copy(out_all, out_hbm, out_sem.at[0])]
    stores.append(pltpu.make_async_copy(gp_all, gp_hbm, out_sem.at[1]))
    for store in stores:
        store.start()
    inv = jnp.concatenate([degree[...]] * (width // LANES), axis=1)
    gs_all[...] = (mm(gp_all[...], wn[...], ((1,), (1,))) * inv).astype(BF16)
    stores.append(pltpu.make_async_copy(gs_all, gs_hbm, out_sem.at[2]))
    stores[-1].start()
    me = lax.axis_index("dom")
    *keeps, send = chain_all
    share = send.shape[2]
    places = [(ref, p) for ref in keeps for p in range(ref.shape[1])]
    for chain, x in enumerate((agg_all, feat)):
        acc[...] = mm(x[...], gp_all[...], ((0,), (0,)))
        for p, mask in enumerate(masks[chain]):
            mine = jnp.bitwise_xor(me, mask)
            other = jnp.bitwise_xor(me, mask + 1)
            keep, at = places[p]
            keep[chain, at] = acc[pl.ds(pl.multiple_of(mine * share, 8), share), :]
            send[chain, p] = acc[pl.ds(pl.multiple_of(other * share, 8), share), :].astype(BF16)
        for i, (a, b) in enumerate(zip(chain_all, chain_hbm)):
            stores.append(pltpu.make_async_copy(a.at[chain], b.at[chain], chain_sem.at[chain, i]))
            stores[-1].start()
    pack_grads(caps, mm(bnd[...], gs_all[...], ((0,), (0,))), back_all)
    stores.append(pltpu.make_async_copy(back_all, back_hbm, back_sem))
    stores[-1].start()
    for store in stores:
        store.wait()


def stage_one_kernel(keep_ref, core_ref, a_ref, b_ref, token_ref):
    token_ref[...] = jnp.zeros_like(token_ref)
    for chain, ref in ((0, a_ref), (1, b_ref)):
        ref[...] = (keep_ref[chain] + core_ref[chain].astype(F32)).astype(BF16)


def stage_two_kernel(keep_ref, core_ref, a1_ref, b1_ref, _, a_ref, b_ref):
    for chain, got, ref in ((0, a1_ref, a_ref), (1, b1_ref, b_ref)):
        total = keep_ref[chain] + core_ref[chain].astype(F32) + got[...].astype(F32)
        ref[...] = total.astype(BF16)


def stage_z_kernel(keep_ref, core_ref, a1_ref, b1_ref, a2_ref, b2_ref, token_ref, base_ref, *outs):
    token_ref[...] = jnp.zeros_like(token_ref)
    for chain, one, two in ((0, a1_ref, a2_ref), (1, b1_ref, b2_ref)):
        total = keep_ref[chain] + core_ref[chain].astype(F32)
        total = total + one[...].astype(F32) + two[...].astype(F32)
        base_ref[chain] = total[0]
        for z, ref in enumerate(outs):
            ref[chain] = total[z + 1].astype(BF16)


def stage_last_kernel(base_ref, z1_ref, z2_ref, z3_ref, neigh_ref, self_ref):
    for chain, ref in ((0, neigh_ref), (1, self_ref)):
        total = base_ref[chain] + z1_ref[chain].astype(F32)
        ref[...] = total + z2_ref[chain].astype(F32) + z3_ref[chain].astype(F32)


def own_kernel(send_ref, count_ref, gp_ref, w_ref, own_t_ref, gs_ref, _, out_ref, place_ref, token_ref, hits):
    token_ref[...] = jnp.zeros_like(token_ref)
    out_ref[...] = mm(gp_ref[...], w_ref[...], ((1,), (1,))) + mm(own_t_ref[...], gs_ref[...])
    caps, parts = send_ref.shape
    here = hits.shape[1]
    idx = slot_indices(send_ref, count_ref) - pl.program_id(0) * here
    lane = lax.broadcasted_iota(jnp.int32, (caps, here), 1)
    for d in range(parts):
        hit = jnp.where(lane == idx[:, d : d + 1], 1.0, 0.0)
        hits[d * caps : (d + 1) * caps, :] = hit.astype(BF16)
    place_ref[...] = hits[...].T


def final_kernel(caps, hub_ref, own_ref, got_ref, place_ref, out_ref, token_ref, rows):
    token_ref[...] = jnp.zeros_like(token_ref)
    step = pl.program_id(0)
    parts = got_ref.shape[0]
    bnd = parts * caps
    here, width = out_ref.shape
    groups = width // LANES

    @pl.when(step == 0)
    def _():
        for g in range(groups):
            piece = got_ref[:, g * caps : (g + 1) * caps, :]
            rows[:, g * LANES : (g + 1) * LANES] = piece.reshape(bnd, LANES)

    out_ref[...] = own_ref[...] + mm(place_ref[...], rows[...])
    hubs = jnp.sum(got_ref[:, groups * caps :, :].astype(F32), axis=0)
    for i in range(4):
        row = jnp.concatenate([hubs[4 * g + i : 4 * g + i + 1] for g in range(groups)], axis=1)
        at = hub_ref[0, i] - step * here

        @pl.when((at >= 0) & (at < here))
        def _():
            out_ref[pl.ds(at, 1), :] += row


def swap(x, mask, parts):
    return lax.ppermute(x, "dom", [(d, d ^ mask) for d in range(parts)])


VMEM = pl.BlockSpec(memory_space=pltpu.VMEM)
SMEM = pl.BlockSpec(memory_space=pltpu.SMEM)
ANY = pl.BlockSpec(memory_space=pl.ANY)


def on_device_fast(
    features,
    w_self,
    w_neigh,
    cotangent,
    tiles,
    tile_src,
    tile_count,
    send_rows,
    send_count,
    hub_rows,
):
    parts = lax.axis_size("dom")
    rows, width = features.shape
    hidden = w_self.shape[1]
    blocks, slots, tile, _ = tiles.shape
    caps = send_rows.shape[2]
    hub_own = hub_rows.shape[1]
    bnd = parts * caps
    far = bnd + parts * hub_own
    groups = width // LANES
    sent_rows = groups * (caps + hub_own)
    shape = jax.ShapeDtypeStruct

    send_t = send_rows[0].T

    outgoing = pl.pallas_call(
        pack_kernel,
        out_shape=shape((parts, sent_rows, LANES), BF16),
        in_specs=[VMEM, VMEM, SMEM, VMEM],
        out_specs=VMEM,
        scratch_shapes=[pltpu.VMEM((bnd + 16, rows), BF16)],
        compiler_params=params(LIMIT),
        cost_estimate=cost(2 * bnd * rows * width, 4 * MIB),
        name="pack",
    )(send_t, send_count, hub_rows, features)
    got = lax.all_to_all(outgoing, "dom", split_axis=0, concat_axis=0, tiled=True)

    steps = 4
    per = rows // steps
    row_block = lambda n: pl.BlockSpec((per, n), lambda s: (s, 0))
    col_block = lambda n: pl.BlockSpec((n, per), lambda s: (0, s))
    whole = lambda *n: pl.BlockSpec(n, lambda s: (0,) * len(n))
    bnd_adj, own_adj_t, numer, degree = pl.pallas_call(
        early_kernel,
        grid=(steps,),
        out_shape=(
            shape((rows, far), BF16),
            shape((rows, rows), BF16),
            shape((rows, width), F32),
            shape((rows, LANES), F32),
        ),
        in_specs=[
            SMEM,
            SMEM,
            pl.BlockSpec((blocks // steps, slots, tile, tile), lambda s: (s, 0, 0, 0)),
            whole(rows, width),
        ],
        out_specs=(row_block(far), col_block(rows), row_block(width), row_block(LANES)),
        scratch_shapes=[pltpu.VMEM((per, rows + far), F32)],
        compiler_params=params(LIMIT),
        cost_estimate=cost(6 * 10**9, 16 * MIB),
        name="early",
    )(tile_src, tile_count, tiles, features)

    share = width // parts
    half = parts // 2
    order = lambda first, second: [
        first * (p >> 3) | second * (p >> 2 & 1) | (p & 3) << 3 for p in range(half)
    ]
    outs = [
        shape((rows, hidden), BF16),
        shape((rows, hidden), BF16),
        shape((rows, width), BF16),
        shape((2, 4, share, hidden), F32),
        shape((2, 4, share, hidden), F32),
        shape((2, 8, share, hidden), F32),
        shape((2, half, share, hidden), BF16),
        shape((parts, sent_rows, LANES), BF16),
    ]
    operands = [got, bnd_adj, numer, degree, features, cotangent, w_neigh, w_self]
    layer_out, grad_pre, gs, keep_low, keep_mid, keep_high, send, back = pl.pallas_call(
        functools.partial(main_kernel, caps, (order(4, 2), order(2, 4))),
        out_shape=tuple(outs),
        in_specs=[ANY] + [ANY] * 7,
        out_specs=(ANY,) * 8,
        scratch_shapes=[pltpu.VMEM(a.shape, a.dtype) for a in operands + outs]
        + [
            pltpu.VMEM((far, width + LANES), BF16),
            pltpu.VMEM((rows, hidden), F32),
            pltpu.VMEM((rows, width), BF16),
            pltpu.VMEM((width, hidden), F32),
            pltpu.SemaphoreType.DMA((8,)),
            pltpu.SemaphoreType.DMA((3,)),
            pltpu.SemaphoreType.DMA((2, 4)),
            pltpu.SemaphoreType.DMA(()),
        ],
        compiler_params=params(LIMIT),
        cost_estimate=cost(10**10, 24 * MIB),
        name="middle",
    )(*operands)

    core = swap(send, 1, parts)
    returned = lax.all_to_all(back, "dom", split_axis=0, concat_axis=0, tiled=True)

    both = lambda n, at: pl.BlockSpec((2, n, share, hidden), lambda s: (0, at, 0, 0))
    one = lambda n, at: pl.BlockSpec((n, share, hidden), lambda s: (at, 0, 0))

    def stage(kernel, name, in_specs, out_shape, out_specs, *operands):
        return pl.pallas_call(
            kernel,
            grid=(1,),
            out_shape=out_shape,
            in_specs=in_specs,
            out_specs=out_specs,
            compiler_params=params(12),
            cost_estimate=cost(10**6, 3 * MIB),
            name=name,
        )(*operands)

    halves = shape((half // 2, share, hidden), BF16)
    token = shape((8, LANES), F32)
    token_at = pl.BlockSpec((8, LANES), lambda s: (0, 0))
    a1, b1, sent_one = stage(
        stage_one_kernel,
        "stage_one",
        [both(8, 0), both(8, 1)],
        (halves, halves, token),
        (one(8, 0), one(8, 0), token_at),
        keep_high,
        core,
    )
    got_a1, got_b1 = swap(a1, 4, parts), swap(b1, 2, parts)
    own_grad, place, own_done = pl.pallas_call(
        own_kernel,
        grid=(steps,),
        out_shape=(shape((rows, width), F32), shape((rows, bnd), BF16), token),
        in_specs=[
            VMEM,
            VMEM,
            row_block(hidden),
            whole(width, hidden),
            row_block(rows),
            whole(rows, width),
            ANY,
        ],
        out_specs=(row_block(width), row_block(bnd), token_at),
        scratch_shapes=[pltpu.VMEM((bnd, per), BF16)],
        compiler_params=params(24),
        cost_estimate=cost(4 * 10**9, 10 * MIB),
        name="own",
    )(send_t, send_count, grad_pre, w_self, own_adj_t, gs, sent_one)

    quarters = shape((half // 4, share, hidden), BF16)
    a2, b2 = stage(
        stage_two_kernel,
        "stage_two",
        [both(4, 0), both(4, 1), one(4, 1), one(4, 1), ANY],
        (quarters, quarters),
        (one(4, 0), one(4, 0)),
        keep_mid,
        core,
        got_a1,
        got_b1,
        own_done,
    )
    got_a2, got_b2 = swap(a2, 2, parts), swap(b2, 4, parts)
    pair = shape((2, share, hidden), BF16)
    sent_z, base, *sends = stage(
        stage_z_kernel,
        "stage_z",
        [both(4, 0), both(4, 0), one(4, 0), one(4, 0), one(4, 0), one(4, 0)],
        (token, shape((2, share, hidden), F32), pair, pair, pair),
        (token_at,) + (one(2, 0),) * 4,
        keep_low,
        core,
        got_a1,
        got_b1,
        got_a2,
        got_b2,
    )
    got_z = [swap(sends[z - 1], z << 3, parts) for z in (2, 3, 1)]

    grad_features, final_done = pl.pallas_call(
        functools.partial(final_kernel, caps),
        grid=(steps,),
        out_shape=(shape((rows, width), F32), token),
        in_specs=[SMEM, row_block(width), whole(parts, sent_rows, LANES), row_block(bnd)],
        out_specs=(row_block(width), token_at),
        scratch_shapes=[pltpu.VMEM((bnd, width), BF16)],
        compiler_params=params(LIMIT),
        cost_estimate=cost(10**9, 8 * MIB),
        name="final",
    )(hub_rows, own_grad, returned, place)

    total = shape((share, hidden), F32)
    flat = pl.BlockSpec((share, hidden), lambda s: (0, 0))
    grad_neigh, grad_self = stage(
        stage_last_kernel,
        "stage_last",
        [one(2, 0)] * 4,
        (total, total),
        (flat, flat),
        base,
        *got_z,
    )
    return layer_out, grad_features, grad_self, grad_neigh


def on_device(
    features,
    w_self,
    w_neigh,
    cotangent,
    tiles,
    tile_src,
    tile_count,
    send_rows,
    send_count,
    hub_rows,
):
    groups = lax.axis_size("dom")
    position = lax.axis_index("dom")
    own_rows, width = features.shape
    blocks_own, slots, tile_rows, _ = tiles.shape
    cap_rows = send_rows.shape[2]
    hub_own = hub_rows.shape[1]
    bnd_rows = groups * cap_rows
    hub_total = groups * hub_own
    sources = (own_rows + bnd_rows + hub_total) // tile_rows
    rows_out = send_rows[0]
    counts_out = send_count[0]
    slot_range = jnp.arange(cap_rows, dtype=jnp.int32)
    out_valid = slot_range[None, :] < counts_out[:, None]
    outgoing = jnp.where(out_valid[:, :, None], features[rows_out], jnp.zeros((), jnp.bfloat16))
    boundary, counts_in = (
        lax.all_to_all(outgoing, "dom", split_axis=0, concat_axis=0, tiled=True),
        lax.all_to_all(counts_out[:, None], "dom", split_axis=0, concat_axis=0, tiled=True),
    )
    in_valid = (slot_range[None, :] < counts_in).astype(jnp.float32).reshape(bnd_rows)
    boundary = boundary.reshape(bnd_rows, width)
    hub_mine = features[hub_rows[0]]
    hub_table = lax.all_gather(hub_mine, "dom", axis=0, tiled=True)
    table = jnp.concatenate([features, boundary, hub_table], axis=0)
    valid = jnp.concatenate(
        [jnp.ones((own_rows,), jnp.float32), in_valid, jnp.ones((hub_total,), jnp.float32)]
    )
    table_blocks = table.reshape(sources, tile_rows, width)
    valid_blocks = valid.reshape(sources, tile_rows)
    active = (jnp.arange(slots, dtype=jnp.int32)[None, :] < tile_count[:, None]).astype(jnp.float32)
    column_mask = valid_blocks[tile_src] * active[:, :, None]
    masked = tiles * column_mask[:, :, None, :].astype(jnp.bfloat16)
    picked = table_blocks[tile_src]
    numer = jnp.einsum("tkij,tkjf->tif", masked, picked, preferred_element_type=jnp.float32)
    degree = jnp.sum(masked, axis=(1, 3), dtype=jnp.float32).reshape(own_rows)
    agg = (numer.reshape(own_rows, width) / degree[:, None]).astype(jnp.bfloat16)
    pre = jnp.dot(features, w_self, preferred_element_type=jnp.float32) + jnp.dot(
        agg, w_neigh, preferred_element_type=jnp.float32
    )
    sigmoid_pre = jax.nn.sigmoid(pre)
    layer_out = (pre * sigmoid_pre).astype(jnp.bfloat16)
    grad_pre = (
        cotangent.astype(jnp.float32) * sigmoid_pre * (1.0 + pre * (1.0 - sigmoid_pre))
    ).astype(jnp.bfloat16)
    self_local = jnp.dot(features.T, grad_pre, preferred_element_type=jnp.float32)
    neigh_local = jnp.dot(agg.T, grad_pre, preferred_element_type=jnp.float32)
    self_total, neigh_total = lax.psum((self_local, neigh_local), "dom")
    share = width // groups
    grad_w_self = lax.dynamic_slice_in_dim(self_total, position * share, share, 0)
    grad_w_neigh = lax.dynamic_slice_in_dim(neigh_total, position * share, share, 0)
    grad_scaled = (
        jnp.dot(grad_pre, w_neigh.T, preferred_element_type=jnp.float32) / degree[:, None]
    ).astype(jnp.bfloat16)
    grad_scaled = grad_scaled.reshape(blocks_own, tile_rows, width)
    back_terms = jnp.einsum(
        "tkij,tif->tkjf", masked, grad_scaled, preferred_element_type=jnp.float32
    )
    placement = (
        tile_src[:, :, None] == jnp.arange(sources, dtype=jnp.int32)[None, None, :]
    ).astype(jnp.float32)
    grad_source = jnp.einsum(
        "tks,tkjf->sjf", placement, back_terms, precision=lax.Precision.HIGHEST
    )
    grad_source = grad_source.reshape(sources * tile_rows, width)
    grad_features = (
        jnp.dot(grad_pre, w_self.T, preferred_element_type=jnp.float32) + grad_source[:own_rows]
    )
    bnd_grads = grad_source[own_rows : own_rows + bnd_rows].reshape(groups, cap_rows, width)
    returned = lax.all_to_all(
        bnd_grads.astype(jnp.bfloat16), "dom", split_axis=0, concat_axis=0, tiled=True
    ).astype(bnd_grads.dtype)
    returned = returned * out_valid[:, :, None].astype(jnp.float32)
    grad_features = grad_features.at[rows_out.reshape(-1)].add(returned.reshape(bnd_rows, width))
    hub_back = lax.psum_scatter(
        grad_source[own_rows + bnd_rows :], "dom", scatter_dimension=0, tiled=True
    )
    grad_features = grad_features.at[hub_rows[0]].add(hub_back)
    return (layer_out, grad_features, grad_w_self, grad_w_neigh)


def on_any_device(*args):
    features, send_rows, hub_rows = args[0], args[7], args[9]
    parts = lax.axis_size("dom")
    share = features.shape[1] // parts
    if parts == 32 and share % 8 == 0 and send_rows.shape[2] % 16 == 0 and hub_rows.shape[1] == 4:
        return on_device_fast(*args)
    return on_device(*args)


def solution(mesh):
    in_specs = (
        P("dom", None),
        P(),
        P(),
        P("dom", None),
        P("dom", None, None, None),
        P("dom", None),
        P("dom"),
        P("dom", None, None),
        P("dom", None),
        P("dom", None),
    )
    out_specs = (P("dom", None), P("dom", None), P("dom", None), P("dom", None))
    return jax.shard_map(
        on_any_device, mesh=mesh, in_specs=in_specs, out_specs=out_specs, check_vma=False
    )
```
